32 devices in a mesh: prow: 4 (over y, core), pcol: 8 (over z, x).
Axes of the slice: x: 2, y: 2, z: 4, core: 2. Of those that a mesh axis runs over, the one named last changes fastest.
Arguments:
- rhs: float32 [16, 8, 128, 512], P(None, 'pcol'), may hold values from -6 to 6
- coupling: bfloat16 [16, 8, 32, 4, 128, 128], P(None, 'pcol', None, 'prow'), may hold values from -0.0625 to 0.0625
- pattern: int32 [16, 8, 32, 4], P(None, 'pcol', None, 'prow'), may hold values 0 or 1
- inverse: bfloat16 [4, 4, 8, 8, 4, 128, 128], P(None, None, 'pcol', None, 'prow'), may hold values from -1 to 3
- trail_coupling: bfloat16 [32, 8, 32, 4, 128, 128], P(None, 'pcol', None, 'prow'), may hold values from -0.0625 to 0.0625
- trail_rhs: float32 [32, 8, 128, 512], P('prow', 'pcol'), may hold values from -6 to 6
Outputs:
- solution: bfloat16 [32, 4, 128, 512], P(None, 'prow')
- trail_out: float32 [32, 8, 128, 512], P('prow', 'pcol')
The draws below stay inside these ranges and needn't reach their ends.
Inputs may be any that keep to these rules, and one draw needn't show every extreme that they name: `pattern`: each entry is 1 where the coupling tile is present and 0 where it is empty.
All inputs are finite; a program needn't handle non-finite values. No bound on the sum of `pattern` on one device may be relied on, other than what follows from the above.
Results may differ from the reference program's by a relative error of at most 0.004.
Values may be sent and summed in bfloat16 or wider, within the bound.
No kernel may reach another device: no remote copies, remote signals or barrier semaphores. Data moves between devices by JAX's collectives and lax.ppermute only.
A program may use at most 128 MiB of HBM per device.

```python
import math
import jax
import jax.numpy as jnp
from jax import lax

PANEL = 4096
TB = 128
NP = 4
R = 512
TRAIL = 32768
M = 16384
NT = 128
RT = 16
CT = 32
JT = 4
IT = 8
ST = 32
N_PROW = 4
N_PCOL = 8


def draw_inverse(key, part):
    key = jax.random.fold_in(key, 7)
    draw_shape = (NP, JT, N_PCOL, IT, N_PROW, TB, TB)
    tile_col = lax.broadcasted_iota(jnp.int32, draw_shape, 1) * N_PCOL + lax.broadcasted_iota(jnp.int32, draw_shape, 2)
    tile_row = lax.broadcasted_iota(jnp.int32, draw_shape, 3) * N_PROW + lax.broadcasted_iota(jnp.int32, draw_shape, 4)
    col_index = tile_col * TB + lax.broadcasted_iota(jnp.int32, draw_shape, 5)
    row_index = tile_row * TB + lax.broadcasted_iota(jnp.int32, draw_shape, 6)
    key_diag, key_off = jax.random.split(key)
    diagonal = jnp.exp(jax.random.uniform(key_diag, draw_shape, jnp.float32, math.log(0.5), math.log(2.0)))
    off_values = jnp.clip(jax.random.normal(key_off, draw_shape, jnp.float32), -4.0, 4.0)
    values = jnp.where(row_index == col_index, diagonal, off_values * (0.5 / math.sqrt(PANEL)))
    return values.astype(jnp.bfloat16)


def set_ends(result, rng, smallest, top_value):
    longest = result.shape.index(max(result.shape))
    spots = []
    for shift in (0, 1):
        where = [jax.random.randint(jax.random.fold_in(rng, axis), (), 0, length) for axis, length in enumerate(result.shape)]
        where[longest] = (where[longest] + shift) % result.shape[longest]
        spots.append(tuple(where))
    return result.at[spots[0]].set(smallest).at[spots[1]].set(top_value)


def strengthened(result, rng, source, target, blocks, factor):
    owner, partner = [(jnp.arange(result.shape[position]) // (result.shape[position] // blocks)).reshape([-1 if axis == position else 1 for axis in range(result.ndim)]) for position in (source, target)]
    chosen = jax.random.permutation(rng, blocks)[partner]
    strong = (owner == chosen) | (owner == (partner + blocks // 2) % blocks)
    return jnp.where(strong, factor * result, result)


def block_scale(key, dims, shards, smallest, largest):
    level, own = 1.0, jax.random.fold_in(key, 6)
    for axis_at, blocks in shards:
        steps = jnp.exp(jax.random.uniform(jax.random.fold_in(own, axis_at), (blocks,), jnp.float32, smallest / len(shards), largest / len(shards)))
        level = level * jnp.repeat(steps, dims[axis_at] // blocks).reshape([-1 if axis == axis_at else 1 for axis in range(len(dims))])
    return level


def noise(key, extent, deviation, limit, pieces=(), kind=jnp.bfloat16):
    factor_of = block_scale(key, extent, pieces, -0.22, 0.18) if pieces else 1.0
    entries = jax.random.normal(key, extent, jnp.float32) * deviation * factor_of
    return jnp.minimum(jnp.maximum(entries, -limit), limit).astype(kind)


def bell_draw_with(own_key, dims, spread, reach, cuts, heavy, dtype=jnp.bfloat16):
    values = spread * jax.random.normal(own_key, dims, jnp.float32)
    if cuts:
        values = values * block_scale(own_key, dims, cuts, -0.22, 0.18)
    return jnp.clip(strengthened(values, jax.random.fold_in(own_key, 3), *heavy), -reach, reach).astype(dtype)


def setup_inputs(seed: int = 0) -> dict:
    key_of = jax.random.split(jax.random.key(seed), 7)
    return {
        "rhs": noise(key_of[0], (RT, N_PCOL, TB, R), 1.0, 6.0, ((1, 8),), jnp.float32),
        "coupling": noise(key_of[1], (RT, N_PCOL, CT, N_PROW, TB, TB), (M // 2) ** -0.5, 0.0625, ((1, 8), (3, 4))),
        "pattern": set_ends((jax.random.randint(key_of[2], (RT, N_PCOL, CT, N_PROW), 0, 2) < 1).astype(jnp.int32), jax.random.fold_in(key_of[2], 1), 0, 1),
        "inverse": draw_inverse(jax.random.fold_in(key_of[6], 71), 0),
        "trail_coupling": bell_draw_with(key_of[4], (ST, N_PCOL, CT, N_PROW, TB, TB), M ** -0.5, 0.0625, ((1, 8), (3, 4)), (3, 0, 4, 2.0)),
        "trail_rhs": noise(key_of[5], (ST, N_PCOL, TB, R), 1.0, 6.0, ((0, 4), (1, 8)), jnp.float32),
    }


def reference(rhs, coupling, pattern, inverse, trail_coupling, trail_rhs):
    tile_mask = pattern.reshape(NT, NT).astype(jnp.bfloat16)
    tile_grid = coupling.reshape(NT, NT, TB, TB) * tile_mask[:, :, None, None]
    dense_factor = tile_grid.transpose(0, 2, 1, 3).reshape(M, M)
    rhs_all = rhs.reshape(M, R)
    inverse_blocks = inverse.reshape(NP, PANEL // TB, PANEL // TB, TB, TB).transpose(0, 2, 4, 1, 3).reshape(NP, PANEL, PANEL)
    solved = []
    for panel_index in range(NP):
        row_lower = panel_index * PANEL
        reduced = rhs_all[row_lower:row_lower + PANEL]
        if panel_index > 0:
            known_rows = jnp.concatenate(solved, 0)
            reduced = reduced - jnp.dot(dense_factor[row_lower:row_lower + PANEL, :row_lower], known_rows, preferred_element_type=jnp.float32)
        current = jnp.dot(inverse_blocks[panel_index].astype(jnp.float32), reduced, precision=lax.Precision.HIGHEST, preferred_element_type=jnp.float32)
        solved.append(current.astype(jnp.bfloat16))
    known_all = jnp.concatenate(solved, 0)

    def trail_row(tile_rows):
        flat_rows = tile_rows.transpose(1, 0, 2).reshape(TB, M)
        return jnp.dot(flat_rows, known_all, preferred_element_type=jnp.float32)

    trail_update = lax.map(trail_row, trail_coupling.reshape(TRAIL // TB, NT, TB, TB))
    trail_out = trail_rhs.reshape(TRAIL, R) - trail_update.reshape(TRAIL, R)
    return known_all.reshape(CT, N_PROW, TB, R), trail_out.reshape(ST, N_PCOL, TB, R)
```

```python
import functools

import jax
import jax.numpy as jnp
from jax import lax
from jax.experimental import pallas as pl
from jax.experimental.pallas import tpu as pltpu
from jax.sharding import PartitionSpec as P

SPLITS = 2
LAG = 5
F32 = jnp.float32
BF16 = jnp.bfloat16
CODE = jnp.int16
EXTRA = 16
TOP = 32000.0
MIB = 1024 * 1024
HBM = pl.BlockSpec(memory_space=pltpu.HBM)
SMEM = pl.BlockSpec(memory_space=pltpu.SMEM)
VMEM = pl.BlockSpec(memory_space=pltpu.VMEM)
ANY = pl.BlockSpec(memory_space=pl.ANY)


def swap(value, axis, count, mask):
    return lax.ppermute(value, axis, [(s, s ^ mask) for s in range(count)])


def shape(dims, dtype):
    return jax.ShapeDtypeStruct(tuple(dims), dtype)


def whole(array):
    return pl.BlockSpec(array.shape, lambda *_: (0,) * array.ndim)


def cost(flops, size):
    return pl.CostEstimate(flops=int(flops), bytes_accessed=int(size), transcendentals=0)


def flat_rows(value):
    return value.reshape(-1, value.shape[-1])


def exponent_of(value):
    top = jnp.max(jnp.max(jnp.abs(value), axis=0, keepdims=True), axis=1, keepdims=True)
    return jnp.ceil(jnp.log2(jnp.maximum(top, 1e-30)))


def encode(value, exponent):
    return jnp.round(value * (TOP * jnp.exp2(-exponent))).astype(jnp.int32).astype(CODE)


def put_exponent(ref, count, exponent):
    ref[count : count + EXTRA] = jnp.broadcast_to(exponent, (EXTRA, ref.shape[1])).astype(jnp.int32).astype(CODE)


def decode(ref):
    count = ref.shape[0] - EXTRA
    tail = ref[count : count + EXTRA].astype(jnp.int32).astype(F32)
    factor = jnp.exp2(tail[:1, :1]) * (1.0 / TOP)
    return ref[:count].astype(jnp.int32).astype(F32) * factor


def tile_matrix(block, scale=None):
    lines = []
    for a in range(block.shape[0]):
        tiles = [block[a, c] for c in range(block.shape[1])]
        if scale is not None:
            tiles = [t * scale(a, c) for c, t in enumerate(tiles)]
        lines.append(jnp.concatenate(tiles, axis=1))
    return jnp.concatenate(lines, axis=0)


def coupling_kernel(panel, inner, refs):
    own_ref, pattern_ref, coupling_ref = refs[:3]
    xs, pieces = refs[3 : 2 + panel], refs[2 + panel : 2 + panel + inner]
    u_ref, newest_ref, blocks, sems = refs[-4:]
    me = own_ref[0]
    row_count, col_count, tile, _ = blocks.shape[1:]
    copies = []
    for e in range(panel):
        source = coupling_ref.at[pl.ds(panel * row_count, row_count), 0, pl.ds(e * col_count, col_count), 0]
        copies.append(pltpu.make_async_copy(source, blocks.at[e], sems.at[e]))
        copies[e].start()
    for d in range(inner):
        newest_ref[:, me ^ d] = pieces[d][...]
    total = None
    for e in range(panel):
        copies[e].wait()
        x = xs[e][...] if e < panel - 1 else flat_rows(newest_ref[...])

        def scale(a, c, e=e):
            m = pattern_ref[panel * row_count + a, e * col_count + c].astype(F32)
            return jnp.full((tile, tile), m, F32).astype(BF16)

        part = jnp.dot(tile_matrix(blocks.at[e], scale), x, preferred_element_type=F32)
        total = part if total is None else total + part
    u_ref[...] = total


def merge_kernel(coded, refs):
    value_ref, arrived, sum_ref, out_ref = refs[0], refs[1:-2], refs[-2], refs[-1]
    total = value_ref[...]
    for r in arrived:
        total = total + (decode(r) if coded else r[...])
    sum_ref[...] = total
    count = total.shape[0]
    exponent = exponent_of(total)
    out_ref[:count] = encode(total, exponent)
    put_exponent(out_ref, count, exponent)


def inverse_kernel(panel, half, updates, inner, refs):
    own_ref, rhs_ref, inverse_ref = refs[:3]
    rest, (rhs_block, block, sems) = refs[3:-3], refs[-3:]
    row_count, _, width = rhs_block.shape
    source = rhs_ref.at[pl.ds(panel * row_count, row_count), 0, :, pl.ds(half * width, width)]
    get_rhs = pltpu.make_async_copy(source, rhs_block, sems.at[0])
    get_rhs.start()
    get_block = pltpu.make_async_copy(inverse_ref.at[panel, :, 0, :, 0], block, sems.at[1])
    get_block.start()
    get_rhs.wait()
    y = flat_rows(rhs_block[...])
    if updates:
        y = y - rest[0][...]
        for r in rest[1:updates]:
            y = y - decode(r)
        rest = rest[updates:]
    kept_ref, sent, terms_ref = rest[0], rest[1:-1], rest[-1]
    me = own_ref[0]
    high = y.astype(BF16)
    low = (y - high.astype(F32)).astype(BF16)
    get_block.wait()
    out = lax.dot_general(
        tile_matrix(block),
        jnp.concatenate([high, low], axis=1),
        (((0,), (0,)), ((), ())),
        preferred_element_type=F32,
    )
    terms = out[:, :width] + out[:, width:]
    exponent = exponent_of(terms)
    terms_ref[...] = terms.reshape(terms_ref.shape)
    outer, _, rows, _ = terms_ref.shape
    for o in range(outer):
        kept_ref[o] = terms_ref[o, me]
        for d, ref in enumerate(sent):
            ref[o * rows : (o + 1) * rows] = encode(terms_ref[o, me ^ (d + 1)], exponent)
    for ref in sent:
        put_exponent(ref, outer * rows, exponent)


def fold_kernel(inner, outer, refs):
    own_ref, kept_ref, arrived = refs[0], refs[1], refs[2 : 1 + inner]
    mine_ref, sent, total_ref = refs[-1 - outer], refs[-outer:-1], refs[-1]
    me = own_ref[0]
    total = flat_rows(kept_ref[...])
    for r in arrived:
        total = total + decode(r)
    exponent = exponent_of(total)
    total_ref[...] = total.reshape(total_ref.shape)
    rows = total_ref.shape[1]
    mine_ref[...] = total_ref[me]
    for d, ref in enumerate(sent):
        ref[:rows] = encode(total_ref[me ^ (d + 1)], exponent)
        put_exponent(ref, rows, exponent)


def finish_kernel(refs):
    total = refs[0][...]
    for r in refs[1:-1]:
        total = total + decode(r)
    refs[-1][...] = total.astype(BF16)


def order_kernel(refs):
    me, out_ref = refs[0][0], refs[-1]
    for d, piece in enumerate(refs[1:-1]):
        out_ref[me ^ d] = piece[...]


def order_last_kernel(refs):
    me, out_ref = refs[0][0], refs[-1]
    for d, piece in enumerate(refs[1:-1]):
        out_ref[:, me ^ d] = piece[...]


def trail_kernel(groups, add, refs):
    blocks, rest, out_ref = refs[1 : 1 + groups], refs[1 + groups : -1], refs[-1]
    count = (len(rest) - int(add)) // groups
    total = flat_rows(rest[-1][...]) if add else None
    for g in range(groups):
        xs = [rest[g * count + i][...] for i in range(count)]
        x = jnp.concatenate(xs, axis=1) if count > 1 else xs[0]
        part = jnp.dot(tile_matrix(blocks[g]), x, preferred_element_type=F32)
        total = part if total is None else total + part
    out_ref[...] = total.astype(out_ref.dtype).reshape(out_ref.shape)


def add_kernel(refs):
    total = refs[0][...]
    for r in refs[1:-1]:
        total = total + r[...].astype(F32)
    refs[-1][...] = total.astype(refs[-1].dtype)


def join_kernel(count, refs):
    out_ref = refs[-1]
    halves = refs[:count]
    width = halves[0].shape[-1]
    for i, r in enumerate(halves):
        out_ref[:, i * width : (i + 1) * width] = r[...]


def subtract_kernel(count, refs):
    total = refs[0][...]
    for r in refs[1:count]:
        total = total - r[...].astype(F32)
    refs[-1][...] = total


def make_body(nr, nc):
    cores = 2 if nr % 2 == 0 else 1
    lines = nr // cores
    outer = min(nc, 4)
    inner = nc // outer

    def body(rhs, coupling, pattern, inverse, trail_coupling, trail_rhs):
        rhs = pltpu.with_memory_space_constraint(rhs, pltpu.HBM)
        coupling = pltpu.with_memory_space_constraint(coupling, pltpu.HBM)
        inverse = pltpu.with_memory_space_constraint(inverse, pltpu.HBM)
        row_index = lax.axis_index("prow")
        col_index = lax.axis_index("pcol")
        core, line = row_index % cores, row_index // cores
        inner_own = jnp.reshape(col_index % inner, (1,))
        outer_own = jnp.reshape(col_index // inner, (1,))
        panels, row_count, _, col_count = inverse.shape[:4]
        tile, width = rhs.shape[2:]
        part = width // SPLITS
        rows = col_count * tile // nc
        reduced_rows = row_count * tile
        solved_dims = (col_count * tile, part)
        trail_tiles = trail_coupling.shape[0]
        group = trail_tiles // nr
        step_tiles = min(4, group)
        pattern_flat = pattern.reshape(pattern.shape[0], pattern.shape[2])
        last = [None]

        def call(kernel, operands, specs, outs, name, flops=0, size=0, scratch=(), limit=12):
            operands, specs = list(operands), list(specs)
            extra = 0
            if last[0] is not None:
                operands.append(last[0])
                specs.append(ANY)
                extra = 1
            count = len(operands)

            def run(*refs):
                kernel(refs[: count - extra] + refs[count:])

            result = pl.pallas_call(
                run,
                in_specs=specs,
                out_specs=[VMEM] * len(outs),
                out_shape=outs,
                scratch_shapes=list(scratch),
                compiler_params=pltpu.CompilerParams(vmem_limit_bytes=limit * MIB),
                cost_estimate=cost(1, 1),
                name=name,
            )(*operands)
            last[0] = result[0]
            return result

        def couple(k, h, older, pieces):
            outs = [shape((reduced_rows, part), F32), shape((outer, inner, rows, part), BF16)]
            return call(
                functools.partial(coupling_kernel, k, inner),
                [inner_own, pattern_flat, coupling] + older + pieces,
                [SMEM, SMEM, HBM] + [VMEM] * len(older + pieces),
                outs,
                "coupling",
                2 * reduced_rows * k * col_count * tile * part,
                2 * k * reduced_rows * col_count * tile,
                scratch=[
                    pltpu.VMEM((k, row_count, col_count, tile, tile), BF16),
                    pltpu.SemaphoreType.DMA((k,)),
                ],
                limit=24,
            )

        def merge(value, arrived, coded):
            outs = [shape(value.shape, F32), shape((value.shape[0] + EXTRA, part), CODE)]
            return call(
                functools.partial(merge_kernel, coded),
                [value] + arrived,
                [VMEM] * (1 + len(arrived)),
                outs,
                "merge",
                size=10 * value.size,
            )

        def invert(k, h, update):
            outs = [shape((outer, rows, part), F32)]
            outs += [shape((outer * rows + EXTRA, part), CODE)] * (inner - 1)
            return call(
                functools.partial(inverse_kernel, k, h, len(update), inner),
                [inner_own, rhs, inverse] + update,
                [SMEM, HBM, HBM] + [VMEM] * len(update),
                outs,
                "inverse",
                4 * reduced_rows * col_count * tile * part,
                2 * reduced_rows * col_count * tile,
                scratch=[
                    pltpu.VMEM((outer, inner, rows, part), F32),
                    pltpu.VMEM((row_count, tile, part), F32),
                    pltpu.VMEM((row_count, col_count, tile, tile), BF16),
                    pltpu.SemaphoreType.DMA((2,)),
                ],
                limit=24,
            )

        def fold(kept, arrived):
            return call(
                functools.partial(fold_kernel, inner, outer),
                [outer_own, kept] + arrived,
                [SMEM] + [VMEM] * inner,
                [shape((rows, part), F32)] + [shape((rows + EXTRA, part), CODE)] * (outer - 1),
                "fold",
                size=8 * outer * rows * part,
                scratch=[pltpu.VMEM((outer, rows, part), F32)],
            )

        def finish(kept, arrived):
            return call(
                finish_kernel, [kept] + arrived, [VMEM] * outer, [shape((rows, part), BF16)], "finish", size=4 * outer * rows * part
            )[0]

        def order(pieces):
            return call(
                order_kernel,
                [outer_own] + pieces,
                [SMEM] + [VMEM] * outer,
                [shape((outer, rows, part), BF16)],
                "order",
                size=4 * outer * rows * part,
            )[0]

        def order_last(pieces):
            return call(
                order_last_kernel,
                [inner_own] + pieces,
                [SMEM] + [VMEM] * inner,
                [shape((outer, inner, rows, part), BF16)],
                "order_last",
                size=4 * nc * rows * part,
            )[0]

        def trail_product(first, count, xs, added, rank, columns, dtype, chain=False):
            steps = (trail_tiles if rank is None else group) // step_tiles
            base = jnp.reshape(0 if rank is None else rank * steps, (1,)).astype(jnp.int32)
            wide = width if columns is None else part
            column = 0 if columns is None else columns
            operands = [trail_coupling] * count + xs + ([] if added is None else [added])
            specs = [
                pl.BlockSpec(
                    (step_tiles, None, col_count, None, tile, tile),
                    functools.partial(lambda g, i, b: (b[0] + i, 0, g, 0, 0, 0), first + g),
                )
                for g in range(count)
            ] + [whole(v) for v in xs]
            if added is not None:
                specs.append(pl.BlockSpec((step_tiles, tile, wide), lambda i, b: (b[0] + i, 0, column)))
            extra = int(chain)
            if chain:
                operands.append(last[0])
                specs.append(ANY)
            total = 1 + len(operands)

            def run(*refs):
                trail_kernel(count, added is not None, refs[: total - extra] + refs[total:])

            result = pl.pallas_call(
                run,
                grid_spec=pltpu.PrefetchScalarGridSpec(
                    num_scalar_prefetch=1,
                    grid=(steps,),
                    in_specs=specs,
                    out_specs=pl.BlockSpec((step_tiles, tile, wide), lambda i, b: (i, 0, 0)),
                ),
                out_shape=shape((steps * step_tiles, tile, wide), dtype),
                compiler_params=pltpu.CompilerParams(vmem_limit_bytes=36 * MIB),
                cost_estimate=cost(
                    2 * steps * step_tiles * tile * count * col_count * tile * wide,
                    steps * step_tiles * tile * (2 * count * col_count * tile + 4 * wide),
                ),
                name="trail",
            )(base, *operands)
            if chain:
                last[0] = result
            return result

        def add(values, dtype, name):
            return call(
                add_kernel, values, [VMEM] * len(values), [shape(values[0].shape, dtype)], name, size=10 * values[0].size
            )[0]

        def join(known, first, count):
            operands, specs = [], []
            for h in range(SPLITS):
                if count > 1:
                    operands.append(jnp.stack([solved[h][first + i] for i in range(count)]))
                else:
                    operands.append(solved[h][first][None])
                specs.append(pl.BlockSpec((None,) + solved_dims, lambda i: (i, 0, 0)))
            aliases = {}
            if known is not None:
                operands.append(known)
                specs.append(ANY)
                aliases = {SPLITS: 0}
            return pl.pallas_call(
                lambda *refs: join_kernel(SPLITS, refs),
                grid=(count,),
                in_specs=specs,
                out_specs=pl.BlockSpec((None, solved_dims[0], width), lambda i: (first + i, 0, 0)),
                out_shape=shape((panels, solved_dims[0], width), BF16),
                input_output_aliases=aliases,
                compiler_params=pltpu.CompilerParams(vmem_limit_bytes=36 * MIB),
                cost_estimate=cost(0, 4 * count * solved_dims[0] * width),
                name="join",
            )(*operands)

        def subtract(out, h, values):
            operands = [trail_rhs] + values
            half = pl.BlockSpec((group, None, tile, part), lambda *_: (0, 0, 0, h))
            specs = [half] + [whole(v) for v in values]
            aliases = {}
            if out is not None:
                aliases = {len(operands): 0}
                operands.append(out)
                specs.append(ANY)
            count = 1 + len(values)
            return pl.pallas_call(
                lambda *refs: subtract_kernel(count, refs),
                grid=(1,),
                in_specs=specs,
                out_specs=half,
                out_shape=shape(trail_rhs.shape, F32),
                input_output_aliases=aliases,
                compiler_params=pltpu.CompilerParams(vmem_limit_bytes=36 * MIB),
                cost_estimate=cost(0, 12 * group * tile * part),
                name="subtract",
            )(*operands)

        solved = [[] for _ in range(SPLITS)]
        trail_sums = [None] * SPLITS
        trail = [None]

        def chain_of(h):
            pieces = None
            for k in range(panels):
                update = []
                if k > 0:
                    u, newest = couple(k, h, solved[h], pieces)
                    solved[h].append(newest.reshape(solved_dims))
                    arrived = [swap(u, "prow", nr, d) for d in range(1, cores)]
                    yield
                    update, message = merge(u, arrived, False)
                    d = 1
                    while d < lines:
                        arrived = swap(message, "prow", nr, d * cores)
                        yield
                        d *= 2
                        if d < lines:
                            update, message = merge(update, [arrived], True)
                    update = [update] + ([arrived] if lines > 1 else [])
                kept, *sent = invert(k, h, update)
                arrived = [swap(v, "pcol", nc, d + 1) for d, v in enumerate(sent)]
                yield
                kept, *sent = fold(kept, arrived)
                arrived = [swap(v, "pcol", nc, (d + 1) * inner) for d, v in enumerate(sent)]
                yield
                mine = finish(kept, arrived)
                arrived = [swap(mine, "pcol", nc, d * inner) for d in range(1, outer)]
                yield
                column = order([mine] + arrived)
                pieces = [column] + [swap(column, "pcol", nc, d) for d in range(1, inner)]
                yield
            solved[h].append(order_last(pieces).reshape(solved_dims))

            def rows_of(rank, dtype):
                return trail_product(panels - 1, 1, [solved[h][-1]], trail[0], rank, h, dtype, True)

            received = []
            for e in list(range(1, lines)) + [0]:
                there = line ^ e
                sent = [rows_of(there * cores + (core ^ d), BF16) for d in range(1, cores)]
                total = rows_of(there * cores + core, F32)
                arrived = [swap(v, "prow", nr, d + 1) for d, v in enumerate(sent)]
                if e == 0:
                    trail_sums[h] = [total] + arrived + received
                else:
                    received.append(swap(add([total] + arrived, BF16, "add"), "prow", nr, e * cores))
                yield

        chains = [chain_of(h) for h in range(SPLITS)]
        alive = [True] * SPLITS
        step = 0
        while any(alive):
            for h in range(SPLITS):
                if alive[h] and step >= h * LAG:
                    alive[h] = next(chains[h], "end") != "end"
            step += 1
            if trail[0] is None and all(len(s) == panels - 1 for s in solved):
                done = panels - 1
                xs = [solved[h][e] for e in range(done) for h in range(SPLITS)]
                trail[0] = trail_product(0, done, xs, None, None, None, F32)

        known = join(None, 0, panels - 1)
        known = join(known, panels - 1, 1)
        trail_out = None
        for h in range(SPLITS):
            trail_out = subtract(trail_out, h, trail_sums[h])
        return known.reshape(panels * col_count, 1, tile, width), trail_out

    return body


def solution(mesh):
    placed = (
        P(None, "pcol", None, None),
        P(None, "pcol", None, "prow", None, None),
        P(None, "pcol", None, "prow"),
        P(None, None, "pcol", None, "prow", None, None),
        P(None, "pcol", None, "prow", None, None),
        P("prow", "pcol", None, None),
    )
    return jax.shard_map(
        make_body(mesh.shape["prow"], mesh.shape["pcol"]),
        mesh=mesh,
        in_specs=placed,
        out_specs=(P(None, "prow", None, None), P("prow", "pcol", None, None)),
        check_vma=False,
    )
```

```python
import functools

import jax
import jax.numpy as jnp
from jax import lax
from jax.experimental import pallas as pl
from jax.experimental.pallas import tpu as pltpu
from jax.sharding import PartitionSpec as P

SPLITS = 2
LAG = 2
MERGED = False
PAUSE = 1
F32 = jnp.float32
BF16 = jnp.bfloat16
CODE = jnp.int16
EXTRA = 16
TOP = 32000.0
MIB = 1024 * 1024
HBM = pl.BlockSpec(memory_space=pltpu.HBM)
SMEM = pl.BlockSpec(memory_space=pltpu.SMEM)
VMEM = pl.BlockSpec(memory_space=pltpu.VMEM)
ANY = pl.BlockSpec(memory_space=pl.ANY)


def swap(value, axis, count, mask):
    return lax.ppermute(value, axis, [(s, s ^ mask) for s in range(count)])


def shape(dims, dtype):
    return jax.ShapeDtypeStruct(tuple(dims), dtype)


def whole(array):
    return pl.BlockSpec(array.shape, lambda *_: (0,) * array.ndim)


def cost(flops, size):
    return pl.CostEstimate(flops=int(flops), bytes_accessed=int(size), transcendentals=0)


def flat_rows(value):
    return value.reshape(-1, value.shape[-1])


def exponent_of(value):
    top = jnp.max(jnp.max(jnp.abs(value), axis=0, keepdims=True), axis=1, keepdims=True)
    return jnp.ceil(jnp.log2(jnp.maximum(top, 1e-30)))


def encode(value, exponent):
    return jnp.round(value * (TOP * jnp.exp2(-exponent))).astype(jnp.int32).astype(CODE)


def put_exponent(ref, count, exponent):
    ref[count : count + EXTRA] = jnp.broadcast_to(exponent, (EXTRA, ref.shape[1])).astype(jnp.int32).astype(CODE)


def decode(ref):
    count = ref.shape[0] - EXTRA
    tail = ref[count : count + EXTRA].astype(jnp.int32).astype(F32)
    factor = jnp.exp2(tail[:1, :1]) * (1.0 / TOP)
    return ref[:count].astype(jnp.int32).astype(F32) * factor


def tile_matrix(block, scale=None):
    lines = []
    for a in range(block.shape[0]):
        tiles = [block[a, c] for c in range(block.shape[1])]
        if scale is not None:
            tiles = [t * scale(a, c) for c, t in enumerate(tiles)]
        lines.append(jnp.concatenate(tiles, axis=1))
    return jnp.concatenate(lines, axis=0)


def coupling_kernel(panel, inner, refs):
    own_ref, pattern_ref, coupling_ref = refs[:3]
    xs, pieces = refs[3 : 2 + panel], refs[2 + panel : 2 + panel + inner]
    u_ref, newest_ref, blocks, sems = refs[-4:]
    me = own_ref[0]
    row_count, col_count, tile, _ = blocks.shape[1:]
    copies = []
    for e in range(panel):
        source = coupling_ref.at[pl.ds(panel * row_count, row_count), 0, pl.ds(e * col_count, col_count), 0]
        copies.append(pltpu.make_async_copy(source, blocks.at[e], sems.at[e]))
        copies[e].start()
    for d in range(inner):
        newest_ref[:, me ^ d] = pieces[d][...]
    total = None
    for e in range(panel):
        copies[e].wait()
        x = xs[e][...] if e < panel - 1 else flat_rows(newest_ref[...])

        def scale(a, c, e=e):
            m = pattern_ref[panel * row_count + a, e * col_count + c].astype(F32)
            return jnp.full((tile, tile), m, F32).astype(BF16)

        part = jnp.dot(tile_matrix(blocks.at[e], scale), x, preferred_element_type=F32)
        total = part if total is None else total + part
    u_ref[...] = total


def merge_kernel(coded, refs):
    value_ref, arrived, sum_ref, out_ref = refs[0], refs[1:-2], refs[-2], refs[-1]
    total = value_ref[...]
    for r in arrived:
        total = total + (decode(r) if coded else r[...])
    sum_ref[...] = total
    count = total.shape[0]
    exponent = exponent_of(total)
    out_ref[:count] = encode(total, exponent)
    put_exponent(out_ref, count, exponent)


def inverse_kernel(panel, half, updates, inner, refs):
    own_ref, rhs_ref, inverse_ref = refs[:3]
    rest, (rhs_block, block, sems) = refs[3:-3], refs[-3:]
    row_count, _, width = rhs_block.shape
    source = rhs_ref.at[pl.ds(panel * row_count, row_count), 0, :, pl.ds(half * width, width)]
    get_rhs = pltpu.make_async_copy(source, rhs_block, sems.at[0])
    get_rhs.start()
    get_block = pltpu.make_async_copy(inverse_ref.at[panel, :, 0, :, 0], block, sems.at[1])
    get_block.start()
    get_rhs.wait()
    y = flat_rows(rhs_block[...])
    if updates:
        y = y - rest[0][...]
        for r in rest[1:updates]:
            y = y - decode(r)
        rest = rest[updates:]
    kept_ref, sent, terms_ref = rest[0], rest[1:-1], rest[-1]
    me = own_ref[0]
    high = y.astype(BF16)
    low = (y - high.astype(F32)).astype(BF16)
    get_block.wait()
    out = lax.dot_general(
        tile_matrix(block),
        jnp.concatenate([high, low], axis=1),
        (((0,), (0,)), ((), ())),
        preferred_element_type=F32,
    )
    terms = out[:, :width] + out[:, width:]
    exponent = exponent_of(terms)
    terms_ref[...] = terms.reshape(terms_ref.shape)
    outer, _, rows, _ = terms_ref.shape
    for o in range(outer):
        kept_ref[o] = terms_ref[o, me]
        for d, ref in enumerate(sent):
            ref[o * rows : (o + 1) * rows] = encode(terms_ref[o, me ^ (d + 1)], exponent)
    for ref in sent:
        put_exponent(ref, outer * rows, exponent)


def fold_kernel(inner, outer, refs):
    own_ref, kept_ref, arrived = refs[0], refs[1], refs[2 : 1 + inner]
    mine_ref, sent, total_ref = refs[-1 - outer], refs[-outer:-1], refs[-1]
    me = own_ref[0]
    total = flat_rows(kept_ref[...])
    for r in arrived:
        total = total + decode(r)
    exponent = exponent_of(total)
    total_ref[...] = total.reshape(total_ref.shape)
    rows = total_ref.shape[1]
    mine_ref[...] = total_ref[me]
    for d, ref in enumerate(sent):
        ref[:rows] = encode(total_ref[me ^ (d + 1)], exponent)
        put_exponent(ref, rows, exponent)


def finish_kernel(refs):
    total = refs[0][...]
    for r in refs[1:-1]:
        total = total + decode(r)
    refs[-1][...] = total.astype(BF16)


def order_kernel(refs):
    me, out_ref = refs[0][0], refs[-1]
    for d, piece in enumerate(refs[1:-1]):
        out_ref[me ^ d] = piece[...]


def order_last_kernel(refs):
    me, out_ref = refs[0][0], refs[-1]
    for d, piece in enumerate(refs[1:-1]):
        out_ref[:, me ^ d] = piece[...]


def trail_kernel(groups, add, refs):
    blocks, rest, out_ref, token_ref = refs[1 : 1 + groups], refs[1 + groups : -2], refs[-2], refs[-1]
    token_ref[...] = jnp.zeros(token_ref.shape, F32)
    count = (len(rest) - int(add)) // groups
    total = flat_rows(rest[-1][...]) if add else None
    for g in range(groups):
        xs = [rest[g * count + i][...] for i in range(count)]
        x = jnp.concatenate(xs, axis=1) if count > 1 else xs[0]
        part = jnp.dot(tile_matrix(blocks[g]), x, preferred_element_type=F32)
        total = part if total is None else total + part
    out_ref[...] = total.astype(out_ref.dtype).reshape(out_ref.shape)


def add_kernel(refs):
    total = refs[0][...]
    for r in refs[1:-1]:
        total = total + r[...].astype(F32)
    refs[-1][...] = total.astype(refs[-1].dtype)


def join_kernel(count, refs):
    out_ref = refs[-1]
    halves = refs[:count]
    width = halves[0].shape[-1]
    for i, r in enumerate(halves):
        out_ref[:, i * width : (i + 1) * width] = r[...]


def subtract_kernel(count, refs):
    total = refs[0][...]
    for r in refs[1:count]:
        total = total - r[...].astype(F32)
    refs[-1][...] = total


def make_body(nr, nc):
    cores = 2 if nr % 2 == 0 else 1
    lines = nr // cores
    outer = min(nc, 4)
    inner = nc // outer

    def body(rhs, coupling, pattern, inverse, trail_coupling, trail_rhs):
        trail_rhs = pltpu.with_memory_space_constraint(trail_rhs, pltpu.HBM)
        row_index = lax.axis_index("prow")
        col_index = lax.axis_index("pcol")
        core, line = row_index % cores, row_index // cores
        inner_own = jnp.reshape(col_index % inner, (1,))
        outer_own = jnp.reshape(col_index // inner, (1,))
        panels, row_count, _, col_count = inverse.shape[:4]
        tile, width = rhs.shape[2:]
        part = width // SPLITS
        rows = col_count * tile // nc
        reduced_rows = row_count * tile
        solved_dims = (col_count * tile, part)
        trail_tiles = trail_coupling.shape[0]
        group = trail_tiles // nr
        pattern_flat = pattern.reshape(pattern.shape[0], pattern.shape[2])
        last = [None]

        def call(kernel, operands, specs, outs, name, flops=0, size=0, scratch=(), limit=12):
            operands, specs = list(operands), list(specs)
            extra = 0
            if last[0] is not None:
                operands.append(last[0])
                specs.append(ANY)
                extra = 1
            count = len(operands)

            def run(*refs):
                kernel(refs[: count - extra] + refs[count:])

            result = pl.pallas_call(
                run,
                in_specs=specs,
                out_specs=[VMEM] * len(outs),
                out_shape=outs,
                scratch_shapes=list(scratch),
                compiler_params=pltpu.CompilerParams(vmem_limit_bytes=limit * MIB),
                cost_estimate=cost(10e9, 1),
                name=name,
            )(*operands)
            last[0] = result[0]
            return result

        def couple(k, h, older, pieces):
            outs = [shape((reduced_rows, part), F32), shape((outer, inner, rows, part), BF16)]
            return call(
                functools.partial(coupling_kernel, k, inner),
                [inner_own, pattern_flat, coupling] + older + pieces,
                [SMEM, SMEM, HBM] + [VMEM] * len(older + pieces),
                outs,
                "coupling",
                2 * reduced_rows * k * col_count * tile * part,
                2 * k * reduced_rows * col_count * tile,
                scratch=[
                    pltpu.VMEM((k, row_count, col_count, tile, tile), BF16),
                    pltpu.SemaphoreType.DMA((k,)),
                ],
                limit=24,
            )

        def merge(value, arrived, coded):
            outs = [shape(value.shape, F32), shape((value.shape[0] + EXTRA, part), CODE)]
            return call(
                functools.partial(merge_kernel, coded),
                [value] + arrived,
                [VMEM] * (1 + len(arrived)),
                outs,
                "merge",
                size=10 * value.size,
            )

        def invert(k, h, update):
            outs = [shape((outer, rows, part), F32)]
            outs += [shape((outer * rows + EXTRA, part), CODE)] * (inner - 1)
            return call(
                functools.partial(inverse_kernel, k, h, len(update), inner),
                [inner_own, rhs, inverse] + update,
                [SMEM, HBM, HBM] + [VMEM] * len(update),
                outs,
                "inverse",
                4 * reduced_rows * col_count * tile * part,
                2 * reduced_rows * col_count * tile,
                scratch=[
                    pltpu.VMEM((outer, inner, rows, part), F32),
                    pltpu.VMEM((row_count, tile, part), F32),
                    pltpu.VMEM((row_count, col_count, tile, tile), BF16),
                    pltpu.SemaphoreType.DMA((2,)),
                ],
                limit=24,
            )

        def fold(kept, arrived):
            return call(
                functools.partial(fold_kernel, inner, outer),
                [outer_own, kept] + arrived,
                [SMEM] + [VMEM] * inner,
                [shape((rows, part), F32)] + [shape((rows + EXTRA, part), CODE)] * (outer - 1),
                "fold",
                size=8 * outer * rows * part,
                scratch=[pltpu.VMEM((outer, rows, part), F32)],
            )

        def finish(kept, arrived):
            return call(
                finish_kernel, [kept] + arrived, [VMEM] * outer, [shape((rows, part), BF16)], "finish", size=4 * outer * rows * part
            )[0]

        def order(pieces):
            return call(
                order_kernel,
                [outer_own] + pieces,
                [SMEM] + [VMEM] * outer,
                [shape((outer, rows, part), BF16)],
                "order",
                size=4 * outer * rows * part,
            )[0]

        def order_last(pieces):
            return call(
                order_last_kernel,
                [inner_own] + pieces,
                [SMEM] + [VMEM] * inner,
                [shape((outer, inner, rows, part), BF16)],
                "order_last",
                size=4 * nc * rows * part,
            )[0]

        def trail_product(first, xs, added, rank, column, dtype):
            count = len(xs)
            step_tiles = min(4, group)
            steps = group // step_tiles
            base = jnp.reshape(rank * steps, (1,)).astype(jnp.int32)
            operands = [trail_coupling] * count + xs + ([] if added is None else [added]) + [last[0]]
            specs = [
                pl.BlockSpec(
                    (step_tiles, None, col_count, None, tile, tile),
                    functools.partial(lambda g, i, b: (b[0] + i, 0, g, 0, 0, 0), first + g),
                )
                for g in range(count)
            ] + [whole(v) for v in xs]
            if added is not None:
                specs.append(pl.BlockSpec((step_tiles, tile, part), lambda i, b: (i, 0, 0)))
            specs.append(ANY)
            total = 1 + len(operands)

            def run(*refs):
                trail_kernel(count, added is not None, refs[: total - 1] + refs[total:])

            token = shape((8, 128), F32)
            result = pl.pallas_call(
                run,
                grid_spec=pltpu.PrefetchScalarGridSpec(
                    num_scalar_prefetch=1,
                    grid=(steps,),
                    in_specs=specs,
                    out_specs=[
                        pl.BlockSpec((step_tiles, tile, part), lambda i, b: (i, 0, 0)),
                        whole(token),
                    ],
                ),
                out_shape=[shape((group, tile, part), dtype), token],
                compiler_params=pltpu.CompilerParams(vmem_limit_bytes=36 * MIB),
                cost_estimate=cost(10e9, 1),
                name="trail",
            )(base, *operands)
            last[0] = result[1]
            return result[0]

        def add(values, dtype, name):
            return call(
                add_kernel, values, [VMEM] * len(values), [shape(values[0].shape, dtype)], name, size=10 * values[0].size
            )[0]

        def join(known, first, count):
            operands, specs = [], []
            for h in range(SPLITS):
                if count > 1:
                    operands.append(jnp.stack([solved[h][first + i] for i in range(count)]))
                else:
                    operands.append(solved[h][first][None])
                specs.append(pl.BlockSpec((None,) + solved_dims, lambda i: (i, 0, 0)))
            aliases = {}
            if known is not None:
                operands.append(known)
                specs.append(ANY)
                aliases = {SPLITS: 0}
            return pl.pallas_call(
                lambda *refs: join_kernel(SPLITS, refs),
                grid=(count,),
                in_specs=specs,
                out_specs=pl.BlockSpec((None, solved_dims[0], width), lambda i: (first + i, 0, 0)),
                out_shape=shape((panels, solved_dims[0], width), BF16),
                input_output_aliases=aliases,
                compiler_params=pltpu.CompilerParams(vmem_limit_bytes=36 * MIB),
                cost_estimate=cost(0, 4 * count * solved_dims[0] * width),
                name="join",
            )(*operands)

        def subtract(out, h, values):
            operands = [trail_rhs] + values
            half = pl.BlockSpec((group, None, tile, part), lambda *_: (0, 0, 0, h))
            specs = [half] + [whole(v) for v in values]
            aliases = {}
            if out is not None:
                aliases = {len(operands): 0}
                operands.append(out)
                specs.append(ANY)
            count = 1 + len(values)
            return pl.pallas_call(
                lambda *refs: subtract_kernel(count, refs),
                grid=(1,),
                in_specs=specs,
                out_specs=half,
                out_shape=shape(trail_rhs.shape, F32),
                input_output_aliases=aliases,
                compiler_params=pltpu.CompilerParams(vmem_limit_bytes=36 * MIB),
                cost_estimate=cost(0, 12 * group * tile * part),
                name="subtract",
            )(*operands)

        solved = [[] for _ in range(SPLITS)]
        trail_sums = [None] * SPLITS

        def chain_of(h):
            pieces = None
            early = {}
            wanted = [(e, d) for e in range(1, lines) for d in list(range(1, cores)) + [0]]

            def begin():
                if h == SPLITS - 1 and k == panels - 1 and wanted:
                    e, d = wanted.pop(0)
                    early[e, d] = trail_product(0, solved[h], None, (line ^ e) * cores + (core ^ d), h, F32)

            for k in range(panels):
                update = []
                if k > 0:
                    u, newest = couple(k, h, solved[h], pieces)
                    solved[h].append(newest.reshape(solved_dims))
                    arrived = [swap(u, "prow", nr, d) for d in range(1, cores)]
                    if not MERGED:
                        yield
                    update, message = merge(u, arrived, False)
                    d = 1
                    while d < lines:
                        arrived = swap(message, "prow", nr, d * cores)
                        begin()
                        yield
                        d *= 2
                        if d < lines:
                            update, message = merge(update, [arrived], True)
                    update = [update] + ([arrived] if lines > 1 else [])
                kept, *sent = invert(k, h, update)
                arrived = [swap(v, "pcol", nc, d + 1) for d, v in enumerate(sent)]
                begin()
                yield
                kept, *sent = fold(kept, arrived)
                arrived = [swap(v, "pcol", nc, (d + 1) * inner) for d, v in enumerate(sent)]
                yield
                mine = finish(kept, arrived)
                arrived = [swap(mine, "pcol", nc, d * inner) for d in range(1, outer)]
                yield
                column = order([mine] + arrived)
                pieces = [column] + [swap(column, "pcol", nc, d) for d in range(1, inner)]
                yield
            solved[h].append(order_last(pieces).reshape(solved_dims))
            received = []
            for e in list(range(1, lines)) + [0]:
                there = line ^ e

                def rows_of(d, dtype):
                    rank = there * cores + (core ^ d)
                    if (e, d) in early:
                        return trail_product(panels - 1, solved[h][-1:], early[e, d], rank, h, dtype)
                    return trail_product(0, solved[h], None, rank, h, dtype)

                arrived = []
                for d in range(1, cores):
                    arrived.append(swap(rows_of(d, BF16), "prow", nr, d))
                    yield
                total = rows_of(0, F32)
                if e == 0:
                    trail_sums[h] = [total] + arrived + received
                else:
                    received.append(swap(add([total] + arrived, BF16, "add"), "prow", nr, e * cores))
                yield
                if e == lines - 1 and h < SPLITS - 1:
                    for _ in range(PAUSE):
                        yield

        chains = [chain_of(h) for h in range(SPLITS)]
        alive = [True] * SPLITS
        step = 0
        while any(alive):
            for h in range(SPLITS):
                if alive[h] and step >= h * LAG:
                    alive[h] = next(chains[h], "end") != "end"
            step += 1
        known = join(None, 0, panels - 1)
        known = join(known, panels - 1, 1)
        trail_out = None
        for h in range(SPLITS):
            trail_out = subtract(trail_out, h, trail_sums[h])
        return known.reshape(panels * col_count, 1, tile, width), trail_out

    return body


def solution(mesh):
    placed = (
        P(None, "pcol", None, None),
        P(None, "pcol", None, "prow", None, None),
        P(None, "pcol", None, "prow"),
        P(None, None, "pcol", None, "prow", None, None),
        P(None, "pcol", None, "prow", None, None),
        P("prow", "pcol", None, None),
    )
    return jax.shard_map(
        make_body(mesh.shape["prow"], mesh.shape["pcol"]),
        mesh=mesh,
        in_specs=placed,
        out_specs=(P(None, "prow", None, None), P("prow", "pcol", None, None)),
        check_vma=False,
    )
```

```python
import functools

import jax
import jax.numpy as jnp
from jax import lax
from jax.experimental import pallas as pl
from jax.experimental.pallas import tpu as pltpu
from jax.sharding import PartitionSpec as P

SPLITS = 2
LAG = 2
MERGED = False
PAUSE = 1
F32 = jnp.float32
BF16 = jnp.bfloat16
CODE = jnp.int16
EXTRA = 16
TOP = 32000.0
MIB = 1024 * 1024
HBM = pl.BlockSpec(memory_space=pltpu.HBM)
SMEM = pl.BlockSpec(memory_space=pltpu.SMEM)
VMEM = pl.BlockSpec(memory_space=pltpu.VMEM)
ANY = pl.BlockSpec(memory_space=pl.ANY)


def swap(value, axis, count, mask):
    return lax.ppermute(value, axis, [(s, s ^ mask) for s in range(count)])


def shape(dims, dtype):
    return jax.ShapeDtypeStruct(tuple(dims), dtype)


def whole(array):
    return pl.BlockSpec(array.shape, lambda *_: (0,) * array.ndim)


def cost(flops, size):
    return pl.CostEstimate(flops=int(flops), bytes_accessed=int(size), transcendentals=0)


def flat_rows(value):
    return value.reshape(-1, value.shape[-1])


def exponent_of(value):
    top = jnp.max(jnp.max(jnp.abs(value), axis=0, keepdims=True), axis=1, keepdims=True)
    return jnp.ceil(jnp.log2(jnp.maximum(top, 1e-30)))


def encode(value, exponent):
    return jnp.round(value * (TOP * jnp.exp2(-exponent))).astype(jnp.int32).astype(CODE)


def put_exponent(ref, count, exponent):
    ref[count : count + EXTRA] = jnp.broadcast_to(exponent, (EXTRA, ref.shape[1])).astype(jnp.int32).astype(CODE)


def decode(ref):
    count = ref.shape[0] - EXTRA
    tail = ref[count : count + EXTRA].astype(jnp.int32).astype(F32)
    factor = jnp.exp2(tail[:1, :1]) * (1.0 / TOP)
    return ref[:count].astype(jnp.int32).astype(F32) * factor


def tile_matrix(block, scale=None):
    lines = []
    for a in range(block.shape[0]):
        tiles = [block[a, c] for c in range(block.shape[1])]
        if scale is not None:
            tiles = [t * scale(a, c) for c, t in enumerate(tiles)]
        lines.append(jnp.concatenate(tiles, axis=1))
    return jnp.concatenate(lines, axis=0)


def coupling_kernel(panel, inner, refs):
    own_ref, pattern_ref, coupling_ref = refs[:3]
    xs, pieces = refs[3 : 2 + panel], refs[2 + panel : 2 + panel + inner]
    u_ref, newest_ref, blocks, sems = refs[-4:]
    me = own_ref[0]
    row_count, col_count, tile, _ = blocks.shape[1:]
    copies = []
    for e in range(panel):
        source = coupling_ref.at[pl.ds(panel * row_count, row_count), 0, pl.ds(e * col_count, col_count), 0]
        copies.append(pltpu.make_async_copy(source, blocks.at[e], sems.at[e]))
        copies[e].start()
    for d in range(inner):
        newest_ref[:, me ^ d] = pieces[d][...]
    total = None
    for e in range(panel):
        copies[e].wait()
        x = xs[e][...] if e < panel - 1 else flat_rows(newest_ref[...])

        def scale(a, c, e=e):
            m = pattern_ref[panel * row_count + a, e * col_count + c].astype(F32)
            return jnp.full((tile, tile), m, F32).astype(BF16)

        part = jnp.dot(tile_matrix(blocks.at[e], scale), x, preferred_element_type=F32)
        total = part if total is None else total + part
    u_ref[...] = total


def merge_kernel(coded, refs):
    value_ref, arrived, sum_ref, out_ref = refs[0], refs[1:-2], refs[-2], refs[-1]
    total = value_ref[...]
    for r in arrived:
        total = total + (decode(r) if coded else r[...])
    sum_ref[...] = total
    count = total.shape[0]
    exponent = exponent_of(total)
    out_ref[:count] = encode(total, exponent)
    put_exponent(out_ref, count, exponent)


def inverse_kernel(panel, half, updates, inner, refs):
    own_ref, rhs_ref, inverse_ref = refs[:3]
    rest, (rhs_block, block, sems) = refs[3:-3], refs[-3:]
    row_count, _, width = rhs_block.shape
    source = rhs_ref.at[pl.ds(panel * row_count, row_count), 0, :, pl.ds(half * width, width)]
    get_rhs = pltpu.make_async_copy(source, rhs_block, sems.at[0])
    get_rhs.start()
    get_block = pltpu.make_async_copy(inverse_ref.at[panel, :, 0, :, 0], block, sems.at[1])
    get_block.start()
    get_rhs.wait()
    y = flat_rows(rhs_block[...])
    if updates:
        y = y - rest[0][...]
        for r in rest[1:updates]:
            y = y - decode(r)
        rest = rest[updates:]
    kept_ref, sent, terms_ref = rest[0], rest[1:-1], rest[-1]
    me = own_ref[0]
    high = y.astype(BF16)
    low = (y - high.astype(F32)).astype(BF16)
    get_block.wait()
    out = lax.dot_general(
        tile_matrix(block),
        jnp.concatenate([high, low], axis=1),
        (((0,), (0,)), ((), ())),
        preferred_element_type=F32,
    )
    terms = out[:, :width] + out[:, width:]
    exponent = exponent_of(terms)
    terms_ref[...] = terms.reshape(terms_ref.shape)
    outer, _, rows, _ = terms_ref.shape
    for o in range(outer):
        kept_ref[o] = terms_ref[o, me]
        for d, ref in enumerate(sent):
            ref[o * rows : (o + 1) * rows] = encode(terms_ref[o, me ^ (d + 1)], exponent)
    for ref in sent:
        put_exponent(ref, outer * rows, exponent)


def fold_kernel(inner, outer, refs):
    own_ref, kept_ref, arrived = refs[0], refs[1], refs[2 : 1 + inner]
    mine_ref, sent, total_ref = refs[-1 - outer], refs[-outer:-1], refs[-1]
    me = own_ref[0]
    total = flat_rows(kept_ref[...])
    for r in arrived:
        total = total + decode(r)
    exponent = exponent_of(total)
    total_ref[...] = total.reshape(total_ref.shape)
    rows = total_ref.shape[1]
    mine_ref[...] = total_ref[me]
    for d, ref in enumerate(sent):
        ref[:rows] = encode(total_ref[me ^ (d + 1)], exponent)
        put_exponent(ref, rows, exponent)


def finish_kernel(refs):
    total = refs[0][...]
    for r in refs[1:-1]:
        total = total + decode(r)
    refs[-1][...] = total.astype(BF16)


def order_kernel(refs):
    me, out_ref = refs[0][0], refs[-1]
    for d, piece in enumerate(refs[1:-1]):
        out_ref[me ^ d] = piece[...]


def order_last_kernel(refs):
    me, out_ref = refs[0][0], refs[-1]
    for d, piece in enumerate(refs[1:-1]):
        out_ref[:, me ^ d] = piece[...]


def trail_kernel(groups, add, refs):
    blocks, rest, out_ref, token_ref = refs[1 : 1 + groups], refs[1 + groups : -2], refs[-2], refs[-1]
    token_ref[...] = jnp.zeros(token_ref.shape, F32)
    count = (len(rest) - int(add)) // groups
    total = flat_rows(rest[-1][...]) if add else None
    for g in range(groups):
        xs = [rest[g * count + i][...] for i in range(count)]
        x = jnp.concatenate(xs, axis=1) if count > 1 else xs[0]
        part = jnp.dot(tile_matrix(blocks[g]), x, preferred_element_type=F32)
        total = part if total is None else total + part
    out_ref[...] = total.astype(out_ref.dtype).reshape(out_ref.shape)


def add_kernel(refs):
    total = refs[0][...]
    for r in refs[1:-1]:
        total = total + r[...].astype(F32)
    refs[-1][...] = total.astype(refs[-1].dtype)


def join_kernel(count, refs):
    out_ref = refs[-1]
    halves = refs[:count]
    width = halves[0].shape[-1]
    for i, r in enumerate(halves):
        out_ref[:, i * width : (i + 1) * width] = r[...]


def subtract_kernel(count, refs):
    total = refs[0][...]
    for r in refs[1:count]:
        total = total - r[...].astype(F32)
    refs[-1][...] = total


def make_body(nr, nc):
    cores = 2 if nr % 2 == 0 else 1
    lines = nr // cores
    outer = min(nc, 4)
    inner = nc // outer

    def body(rhs, coupling, pattern, inverse, trail_coupling, trail_rhs):
        trail_rhs = pltpu.with_memory_space_constraint(trail_rhs, pltpu.HBM)
        row_index = lax.axis_index("prow")
        col_index = lax.axis_index("pcol")
        core, line = row_index % cores, row_index // cores
        inner_own = jnp.reshape(col_index % inner, (1,))
        outer_own = jnp.reshape(col_index // inner, (1,))
        panels, row_count, _, col_count = inverse.shape[:4]
        tile, width = rhs.shape[2:]
        part = width // SPLITS
        rows = col_count * tile // nc
        reduced_rows = row_count * tile
        solved_dims = (col_count * tile, part)
        trail_tiles = trail_coupling.shape[0]
        group = trail_tiles // nr
        pattern_flat = pattern.reshape(pattern.shape[0], pattern.shape[2])
        last = [None]

        def call(kernel, operands, specs, outs, name, flops=0, size=0, scratch=(), limit=12):
            operands, specs = list(operands), list(specs)
            extra = 0
            if last[0] is not None:
                operands.append(last[0])
                specs.append(ANY)
                extra = 1
            count = len(operands)

            def run(*refs):
                kernel(refs[: count - extra] + refs[count:])

            result = pl.pallas_call(
                run,
                in_specs=specs,
                out_specs=[VMEM] * len(outs),
                out_shape=outs,
                scratch_shapes=list(scratch),
                compiler_params=pltpu.CompilerParams(vmem_limit_bytes=limit * MIB),
                cost_estimate=cost(10e9, 1),
                name=name,
            )(*operands)
            last[0] = result[0]
            return result

        def couple(k, h, older, pieces):
            outs = [shape((reduced_rows, part), F32), shape((outer, inner, rows, part), BF16)]
            return call(
                functools.partial(coupling_kernel, k, inner),
                [inner_own, pattern_flat, coupling] + older + pieces,
                [SMEM, SMEM, HBM] + [VMEM] * len(older + pieces),
                outs,
                "coupling",
                2 * reduced_rows * k * col_count * tile * part,
                2 * k * reduced_rows * col_count * tile,
                scratch=[
                    pltpu.VMEM((k, row_count, col_count, tile, tile), BF16),
                    pltpu.SemaphoreType.DMA((k,)),
                ],
                limit=24,
            )

        def merge(value, arrived, coded):
            outs = [shape(value.shape, F32), shape((value.shape[0] + EXTRA, part), CODE)]
            return call(
                functools.partial(merge_kernel, coded),
                [value] + arrived,
                [VMEM] * (1 + len(arrived)),
                outs,
                "merge",
                size=10 * value.size,
            )

        def invert(k, h, update):
            b_all, d_all = rhs, inverse
            if k == 0 and h == 0:
                b_all = pltpu.with_memory_space_constraint(rhs, pltpu.HBM)
                d_all = pltpu.with_memory_space_constraint(inverse, pltpu.HBM)
            outs = [shape((outer, rows, part), F32)]
            outs += [shape((outer * rows + EXTRA, part), CODE)] * (inner - 1)
            return call(
                functools.partial(inverse_kernel, k, h, len(update), inner),
                [inner_own, b_all, d_all] + update,
                [SMEM, HBM, HBM] + [VMEM] * len(update),
                outs,
                "inverse",
                4 * reduced_rows * col_count * tile * part,
                2 * reduced_rows * col_count * tile,
                scratch=[
                    pltpu.VMEM((outer, inner, rows, part), F32),
                    pltpu.VMEM((row_count, tile, part), F32),
                    pltpu.VMEM((row_count, col_count, tile, tile), BF16),
                    pltpu.SemaphoreType.DMA((2,)),
                ],
                limit=24,
            )

        def fold(kept, arrived):
            return call(
                functools.partial(fold_kernel, inner, outer),
                [outer_own, kept] + arrived,
                [SMEM] + [VMEM] * inner,
                [shape((rows, part), F32)] + [shape((rows + EXTRA, part), CODE)] * (outer - 1),
                "fold",
                size=8 * outer * rows * part,
                scratch=[pltpu.VMEM((outer, rows, part), F32)],
            )

        def finish(kept, arrived):
            return call(
                finish_kernel, [kept] + arrived, [VMEM] * outer, [shape((rows, part), BF16)], "finish", size=4 * outer * rows * part
            )[0]

        def order(pieces):
            return call(
                order_kernel,
                [outer_own] + pieces,
                [SMEM] + [VMEM] * outer,
                [shape((outer, rows, part), BF16)],
                "order",
                size=4 * outer * rows * part,
            )[0]

        def order_last(pieces):
            return call(
                order_last_kernel,
                [inner_own] + pieces,
                [SMEM] + [VMEM] * inner,
                [shape((outer, inner, rows, part), BF16)],
                "order_last",
                size=4 * nc * rows * part,
            )[0]

        def trail_product(first, xs, added, rank, column, dtype):
            count = len(xs)
            step_tiles = min(4, group)
            steps = group // step_tiles
            base = jnp.reshape(rank * steps, (1,)).astype(jnp.int32)
            operands = [trail_coupling] * count + xs + ([] if added is None else [added]) + [last[0]]
            specs = [
                pl.BlockSpec(
                    (step_tiles, None, col_count, None, tile, tile),
                    functools.partial(lambda g, i, b: (b[0] + i, 0, g, 0, 0, 0), first + g),
                )
                for g in range(count)
            ] + [whole(v) for v in xs]
            if added is not None:
                specs.append(pl.BlockSpec((step_tiles, tile, part), lambda i, b: (i, 0, 0)))
            specs.append(ANY)
            total = 1 + len(operands)

            def run(*refs):
                trail_kernel(count, added is not None, refs[: total - 1] + refs[total:])

            token = shape((8, 128), F32)
            result = pl.pallas_call(
                run,
                grid_spec=pltpu.PrefetchScalarGridSpec(
                    num_scalar_prefetch=1,
                    grid=(steps,),
                    in_specs=specs,
                    out_specs=[
                        pl.BlockSpec((step_tiles, tile, part), lambda i, b: (i, 0, 0)),
                        whole(token),
                    ],
                ),
                out_shape=[shape((group, tile, part), dtype), token],
                compiler_params=pltpu.CompilerParams(vmem_limit_bytes=36 * MIB),
                cost_estimate=cost(10e9, 1),
                name="trail",
            )(base, *operands)
            last[0] = result[1]
            return result[0]

        def add(values, dtype, name):
            return call(
                add_kernel, values, [VMEM] * len(values), [shape(values[0].shape, dtype)], name, size=10 * values[0].size
            )[0]

        def join(known, first, count):
            operands, specs = [], []
            for h in range(SPLITS):
                if count > 1:
                    operands.append(jnp.stack([solved[h][first + i] for i in range(count)]))
                else:
                    operands.append(solved[h][first][None])
                specs.append(pl.BlockSpec((None,) + solved_dims, lambda i: (i, 0, 0)))
            aliases = {}
            if known is not None:
                operands.append(known)
                specs.append(ANY)
                aliases = {SPLITS: 0}
            return pl.pallas_call(
                lambda *refs: join_kernel(SPLITS, refs),
                grid=(count,),
                in_specs=specs,
                out_specs=pl.BlockSpec((None, solved_dims[0], width), lambda i: (first + i, 0, 0)),
                out_shape=shape((panels, solved_dims[0], width), BF16),
                input_output_aliases=aliases,
                compiler_params=pltpu.CompilerParams(vmem_limit_bytes=36 * MIB),
                cost_estimate=cost(0, 4 * count * solved_dims[0] * width),
                name="join",
            )(*operands)

        def subtract(out, h, values):
            operands = [trail_rhs] + values
            half = pl.BlockSpec((group, None, tile, part), lambda *_: (0, 0, 0, h))
            specs = [half] + [whole(v) for v in values]
            aliases = {}
            if out is not None:
                aliases = {len(operands): 0}
                operands.append(out)
                specs.append(ANY)
            count = 1 + len(values)
            return pl.pallas_call(
                lambda *refs: subtract_kernel(count, refs),
                grid=(1,),
                in_specs=specs,
                out_specs=half,
                out_shape=shape(trail_rhs.shape, F32),
                input_output_aliases=aliases,
                compiler_params=pltpu.CompilerParams(vmem_limit_bytes=36 * MIB),
                cost_estimate=cost(0, 12 * group * tile * part),
                name="subtract",
            )(*operands)

        solved = [[] for _ in range(SPLITS)]
        trail_sums = [None] * SPLITS

        def chain_of(h):
            pieces = None
            early = {}
            wanted = [(e, d) for e in range(1, lines) for d in list(range(1, cores)) + [0]]

            def begin():
                if h == SPLITS - 1 and k == panels - 1 and wanted:
                    e, d = wanted.pop(0)
                    early[e, d] = trail_product(0, solved[h], None, (line ^ e) * cores + (core ^ d), h, F32)

            for k in range(panels):
                update = []
                if k > 0:
                    u, newest = couple(k, h, solved[h], pieces)
                    solved[h].append(newest.reshape(solved_dims))
                    arrived = [swap(u, "prow", nr, d) for d in range(1, cores)]
                    if not MERGED:
                        yield
                    update, message = merge(u, arrived, False)
                    d = 1
                    while d < lines:
                        arrived = swap(message, "prow", nr, d * cores)
                        begin()
                        yield
                        d *= 2
                        if d < lines:
                            update, message = merge(update, [arrived], True)
                    update = [update] + ([arrived] if lines > 1 else [])
                kept, *sent = invert(k, h, update)
                arrived = [swap(v, "pcol", nc, d + 1) for d, v in enumerate(sent)]
                begin()
                yield
                kept, *sent = fold(kept, arrived)
                arrived = [swap(v, "pcol", nc, (d + 1) * inner) for d, v in enumerate(sent)]
                yield
                mine = finish(kept, arrived)
                arrived = [swap(mine, "pcol", nc, d * inner) for d in range(1, outer)]
                yield
                column = order([mine] + arrived)
                pieces = [column] + [swap(column, "pcol", nc, d) for d in range(1, inner)]
                yield
            solved[h].append(order_last(pieces).reshape(solved_dims))
            received = []
            for e in list(range(1, lines)) + [0]:
                there = line ^ e

                def rows_of(d, dtype):
                    rank = there * cores + (core ^ d)
                    if (e, d) in early:
                        return trail_product(panels - 1, solved[h][-1:], early[e, d], rank, h, dtype)
                    return trail_product(0, solved[h], None, rank, h, dtype)

                arrived = []
                for d in range(1, cores):
                    arrived.append(swap(rows_of(d, BF16), "prow", nr, d))
                    yield
                if e == 0 and h < SPLITS - 1:
                    for _ in range(PAUSE):
                        yield
                total = rows_of(0, F32)
                if e == 0:
                    trail_sums[h] = [total] + arrived + received
                else:
                    received.append(swap(add([total] + arrived, BF16, "add"), "prow", nr, e * cores))
                yield

        chains = [chain_of(h) for h in range(SPLITS)]
        alive = [True] * SPLITS
        step = 0
        while any(alive):
            for h in range(SPLITS):
                if alive[h] and step >= h * LAG:
                    alive[h] = next(chains[h], "end") != "end"
            step += 1
        known = join(None, 0, panels - 1)
        known = join(known, panels - 1, 1)
        trail_out = None
        for h in range(SPLITS):
            trail_out = subtract(trail_out, h, trail_sums[h])
        return known.reshape(panels * col_count, 1, tile, width), trail_out

    return body


def solution(mesh):
    placed = (
        P(None, "pcol", None, None),
        P(None, "pcol", None, "prow", None, None),
        P(None, "pcol", None, "prow"),
        P(None, None, "pcol", None, "prow", None, None),
        P(None, "pcol", None, "prow", None, None),
        P("prow", "pcol", None, None),
    )
    return jax.shard_map(
        make_body(mesh.shape["prow"], mesh.shape["pcol"]),
        mesh=mesh,
        in_specs=placed,
        out_specs=(P(None, "prow", None, None), P("prow", "pcol", None, None)),
        check_vma=False,
    )
```
